32 devices in a mesh: ens: 2 (over x), row: 16 (over z, y, core).
Axes of the slice: x: 2, y: 2, z: 4, core: 2. Of those that a mesh axis runs over, the one named last changes fastest.
Arguments:
- jacobian: float32 [32768, 256], P(('ens', 'row')), parts along dimension 0, may hold values from -40 to 40
- residuals: float32 [32768, 128], P(('ens', 'row')), parts along dimension 0, may hold values from -6 to 6
Outputs:
- ortho_basis: float32 [32768, 256], P(('ens', 'row')), parts along dimension 0
- factor: float32 [512, 256], P('ens'), parts along dimension 0
- update: float32 [512, 128], P('ens'), parts along dimension 0
The draws below stay inside these ranges and needn't reach their ends.
There are 2 independent parts, one for each index of `ens`. The reference program is written for one: setup_inputs(seed, part) draws one part's arguments, and reference() takes and returns one part's arrays. A program takes and returns all parts, laid end to end along the dimension named above; each array names one. Nothing has to cross between parts.
All inputs are finite; a program needn't handle non-finite values.
Results may differ from the reference program's by a relative error of at most 0.0003.
Values sent between devices are 32-bit elements; how exact they have to be, the bound alone decides.
A program may use at most 64 MiB of HBM per device.

```python
import math
import jax
import jax.numpy as jnp
from jax import lax

COLS = 256
NRHS = 128
ROWS = 16384


def column_mixing(coupling_key):
    positions = jnp.arange(COLS, dtype=jnp.int32)
    distance = positions[None, :] - positions[:, None]
    decay = 0.5
    above = (distance >= 0).astype(jnp.float32)
    powers = jnp.exp(jnp.maximum(distance, 0).astype(jnp.float32) * math.log(decay)) * above
    first_row = (positions == 0).astype(jnp.float32)
    row_weight = first_row + (1.0 - first_row) * math.sqrt(1.0 - decay * decay)
    local_part = powers * row_weight[:, None]
    block_row = positions // 16
    next_block = (block_row[None, :] == block_row[:, None] + 1).astype(jnp.float32)
    random_blocks = jnp.clip(jax.random.normal(coupling_key, (COLS, COLS), jnp.float32), -3.0, 3.0)
    block_part = jnp.eye(COLS, dtype=jnp.float32) + 0.7 * next_block * random_blocks / 4.0
    return jnp.dot(local_part, block_part, precision=lax.Precision.HIGHEST)


def draw_jacobian(key, part):
    subkeys = jax.random.split(key, 4)
    position = jnp.arange(ROWS, dtype=jnp.float32) / (ROWS - 1)
    spread = jnp.exp(jax.random.uniform(subkeys[1], (ROWS, 1), jnp.float32) * math.log(10.0))
    samples = jnp.clip(jax.random.normal(subkeys[0], (ROWS, COLS), jnp.float32), -5.0, 5.0)
    rising = jnp.exp(position * math.log(3.0))
    row_scale = spread * rising[:, None] * 0.15
    mixing = column_mixing(subkeys[2])
    column_scale = jnp.exp(jax.random.uniform(subkeys[3], (1, COLS), jnp.float32, math.log(0.3), math.log(3.0)))
    mixed_rows = jnp.dot(samples * row_scale, mixing, precision=lax.Precision.HIGHEST)
    return jnp.clip(mixed_rows * column_scale, -40.0, 40.0)


def block_levels(own_key, dims, cuts, least, largest):
    factor_of = 1.0
    for dim, parts in cuts:
        heights = jax.random.uniform(jax.random.fold_in(jax.random.fold_in(own_key, 6), dim), (parts,), jnp.float32, least / len(cuts), largest / len(cuts))
        factor_of = factor_of * jnp.repeat(jnp.exp(heights), dims[dim] // parts).reshape((-1,) + (1,) * (len(dims) - 1 - dim))
    return factor_of


def bell_draw(key, dims, scale, reach, shards=(), kind=jnp.bfloat16):
    entries = jax.random.normal(key, dims, jnp.float32) * scale
    if len(shards) > 0:
        entries = block_levels(key, dims, shards, -0.22, 0.18) * entries
    return jnp.clip(entries, min=-reach, max=reach).astype(kind)


def setup_inputs(seed: int = 0, part: int = 0) -> dict:
    key_of = jax.random.split(jax.random.key(seed), 3)
    part_keys = jax.random.split(jax.random.fold_in(key_of[2], part), 3)
    jacobian = draw_jacobian(jax.random.fold_in(jax.random.fold_in(key_of[2], part), 71), part)
    residuals = bell_draw(part_keys[1], (ROWS, NRHS), 1.0, 6.0, ((0, 16),), jnp.float32)
    return {"jacobian": jacobian, "residuals": residuals}


def cholesky_upper(gram_matrix):
    width = gram_matrix.shape[0]
    positions = jnp.arange(width, dtype=jnp.int32)

    def column_step(column, carry):
        remaining, upper = carry
        onehot = (positions == column).astype(jnp.float32)
        column_values = lax.optimization_barrier(jnp.sum(remaining * onehot[None, :], axis=1))
        pivot_value = jnp.sqrt(jnp.sum(column_values * onehot))
        new_row = column_values / pivot_value * (positions >= column).astype(jnp.float32)
        upper = upper + onehot[:, None] * new_row[None, :]
        remaining = remaining - new_row[:, None] * new_row[None, :]
        return (remaining, upper)
    start = (gram_matrix, jnp.zeros_like(gram_matrix))
    return lax.fori_loop(0, width, column_step, start)[1]

def invert_upper(upper):
    width = upper.shape[0]
    positions = jnp.arange(width, dtype=jnp.int32)

    def row_step(counter, inverse):
        current = width - 1 - counter
        onehot = (positions == current).astype(jnp.float32)
        upper_row = lax.optimization_barrier(jnp.sum(upper * onehot[:, None], axis=0))
        diagonal_entry = jnp.sum(upper_row * onehot)
        product = jnp.dot(upper_row, inverse, precision=lax.Precision.HIGHEST, preferred_element_type=jnp.float32)
        new_row = (onehot - product) / diagonal_entry
        return inverse + onehot[:, None] * new_row[None, :]
    return lax.fori_loop(0, width, row_step, jnp.zeros_like(upper))

def reference(jacobian, residuals):
    precise = lax.Precision.HIGHEST
    contract = (((0,), (0,)), ((), ()))
    gram_matrix = lax.dot_general(jacobian, jacobian, contract, precision=precise, preferred_element_type=jnp.float32) / ROWS
    factor = cholesky_upper(gram_matrix)
    inverse = invert_upper(factor)
    ortho_basis = jnp.dot(jacobian, inverse, precision=precise, preferred_element_type=jnp.float32)
    projected = lax.dot_general(ortho_basis, residuals, contract, precision=precise, preferred_element_type=jnp.float32) / jnp.sqrt(jnp.float32(ROWS))
    update = jnp.dot(inverse, projected, precision=precise, preferred_element_type=jnp.float32)
    return (ortho_basis, factor, update)
```

```python
import jax, jax.numpy as jnp, functools
from jax import lax
from jax.experimental import pallas as pl
from jax.experimental.pallas import tpu as pltpu
HI = lax.Precision.HIGHEST
F32 = jnp.float32

def recip(p):
    return 1.0 / p

def factor_rows(x, extra, first, width):
    nb = x.shape[0]
    diag = []
    mults = []
    rows = [x[8 * i:8 * i + 8] for i in range(nb // 8)]
    ext = [extra[8 * i:8 * i + 8] for i in range(nb // 8)]
    sub = lax.broadcasted_iota(jnp.int32, (8, 128), 0)
    pivots = []
    for p in range(nb // 8):
        cols = []
        for l in range(8):
            c = first + 8 * p + l
            cols.append([jnp.broadcast_to(rows[i][:, c:c + 1], (8, 128)) for i in range(p, nb // 8)])
        pv = jnp.ones((8, 128), F32)
        for j in range(8):
            piv = jnp.broadcast_to(cols[j][0][j:j + 1], (8, 128))
            pv = jnp.where(sub == j, piv, pv)
            r = recip(piv)
            f = [cj * r for cj in cols[j]]
            f[0] = jnp.where(sub > j, f[0], 0.0)
            for l in range(j + 1, 8):
                e = jnp.broadcast_to(cols[l][0][j:j + 1], (8, 128))
                cols[l] = [cl - fi * e for cl, fi in zip(cols[l], f)]
            n = rows[0].shape[1]
            xr = jnp.broadcast_to(rows[p][j:j + 1], (8, n))
            er = jnp.broadcast_to(ext[p][j:j + 1], (8, 128))
            for q, fi in enumerate(f):
                rows[p + q] = rows[p + q] - jnp.concatenate([fi] * (n // 128), axis=1) * xr
                ext[p + q] = ext[p + q] - fi * er
        pivots.append(pv)
    out_r, out_e = [], []
    for i in range(nb // 8):
        s = lax.rsqrt(pivots[i])
        n = rows[0].shape[1]
        out_r.append(rows[i] * jnp.concatenate([s] * (n // 128), axis=1))
        out_e.append(ext[i] * s)
    return jnp.concatenate(out_r, 0), jnp.concatenate(out_e, 0)

def dot(a, b, dims, prec=HI):
    return lax.dot_general(a, b, (dims, ((), ())), precision=prec, preferred_element_type=F32)

def eliminate(blocks, nb):
    n = blocks[0].shape[1]
    count = n // nb
    lane = lax.broadcasted_iota(jnp.int32, (nb, n), 1)
    lane1 = lax.broadcasted_iota(jnp.int32, (nb, 128), 1)
    sub1 = lax.broadcasted_iota(jnp.int32, (nb, 128), 0)
    upper, low = [], []
    for k in range(count):
        off = (k * nb) % 128
        eye = (lane1 == sub1 + off).astype(F32)
        x, e = factor_rows(blocks[k], eye, k * nb, n)
        mine = (lane >= k * nb) & (lane < (k + 1) * nb)
        wide = jnp.concatenate([e] * (n // 128), axis=1)
        t = jnp.where(mine, wide, x)
        urow = lane1[:, :1] * 0 + lax.broadcasted_iota(jnp.int32, (nb, n), 0) + k * nb
        upper.append(jnp.where(lane >= urow, x, 0.0))
        low.append(jnp.where(lane < (k + 1) * nb, t, 0.0))
        if k + 1 < count:
            for i in range(k + 1, count):
                lhs = x[:, i * nb:(i + 1) * nb]
                upd = dot(lhs, t, ((0,), (0,)))
                blocks[i] = jnp.where(mine, 0.0, blocks[i]) - upd
    return upper, low


def factor_kernel(gram_ref, upper_ref, low_ref):
    nb = 32
    n = gram_ref.shape[0]
    blocks = [gram_ref[i * nb:(i + 1) * nb, :] for i in range(n // nb)]
    upper, low = eliminate(blocks, nb)
    for i in range(n // nb):
        upper_ref[i * nb:(i + 1) * nb, :] = upper[i]
        low_ref[i * nb:(i + 1) * nb, :] = low[i]


def shards(jacobian, residuals):
    rows_all = jacobian.shape[0] * lax.axis_size("row")
    gram = dot(jacobian, jacobian, ((0,), (0,))) / rows_all
    data = dot(jacobian, residuals, ((0,), (0,)))
    gram, data = lax.psum((gram, data), "row")
    shape = jax.ShapeDtypeStruct(gram.shape, F32)
    factor, low = pl.pallas_call(factor_kernel, out_shape=(shape, shape),
        compiler_params=pltpu.CompilerParams(vmem_limit_bytes=32 * 1024 * 1024))(gram)
    basis = dot(jacobian, low, ((1,), (1,)))
    projected = dot(low, data, ((1,), (0,))) / jnp.sqrt(jnp.float32(rows_all))
    update = dot(low, projected, ((0,), (0,)))
    return (basis, factor, update)


def solution(mesh):
    from jax.sharding import PartitionSpec as P
    return jax.shard_map(
        shards,
        mesh=mesh,
        in_specs=(P(("ens", "row"), None), P(("ens", "row"), None)),
        out_specs=(P(("ens", "row"), None), P("ens", None), P("ens", None)),
        check_vma=False,
    )
```

```python
import functools
import jax
import jax.numpy as jnp
from jax import lax
from jax.experimental import pallas as pl
from jax.experimental.pallas import tpu as pltpu
from jax.sharding import PartitionSpec as P

HI = lax.Precision.HIGHEST
F32 = jnp.float32

def factor_rows(x, extra, first, width):
    nb = x.shape[0]
    diag = []
    mults = []
    rows = [x[8 * i:8 * i + 8] for i in range(nb // 8)]
    ext = [extra[8 * i:8 * i + 8] for i in range(nb // 8)]
    sub = lax.broadcasted_iota(jnp.int32, (8, 128), 0)
    pivots = []
    for p in range(nb // 8):
        cols = []
        for l in range(8):
            c = first + 8 * p + l
            cols.append([jnp.broadcast_to(rows[i][:, c:c + 1], (8, 128)) for i in range(p, nb // 8)])
        pv = jnp.ones((8, 128), F32)
        for j in range(8):
            piv = jnp.broadcast_to(cols[j][0][j:j + 1], (8, 128))
            pv = jnp.where(sub == j, piv, pv)
            r = 1.0 / piv
            f = [cj * r for cj in cols[j]]
            f[0] = jnp.where(sub > j, f[0], 0.0)
            for l in range(j + 1, 8):
                e = jnp.broadcast_to(cols[l][0][j:j + 1], (8, 128))
                cols[l] = [cl - fi * e for cl, fi in zip(cols[l], f)]
            n = rows[0].shape[1]
            xr = jnp.broadcast_to(rows[p][j:j + 1], (8, n))
            er = jnp.broadcast_to(ext[p][j:j + 1], (8, 128))
            for q, fi in enumerate(f):
                rows[p + q] = rows[p + q] - jnp.concatenate([fi] * (n // 128), axis=1) * xr
                ext[p + q] = ext[p + q] - fi * er
        pivots.append(pv)
    out_r, out_e = [], []
    for i in range(nb // 8):
        s = lax.rsqrt(pivots[i])
        n = rows[0].shape[1]
        out_r.append(rows[i] * jnp.concatenate([s] * (n // 128), axis=1))
        out_e.append(ext[i] * s)
    return jnp.concatenate(out_r, 0), jnp.concatenate(out_e, 0)

def dot(a, b, dims, prec=HI):
    return lax.dot_general(a, b, (dims, ((), ())), precision=prec, preferred_element_type=F32)

def split3(x):
    high = x.astype(jnp.bfloat16)
    rest = x - high.astype(F32)
    middle = rest.astype(jnp.bfloat16)
    return high, middle, (rest - middle.astype(F32)).astype(jnp.bfloat16)


def stacked_product(left, right):
    a, b, c = split3(left)
    d, e, f = split3(right)
    return dot(jnp.concatenate([a, a, b, b, a, c], 0), jnp.concatenate([d, e, d, e, f, d], 0), ((0,), (0,)), None)


def eliminate(blocks, nb):
    n = blocks[0].shape[1]
    count = n // nb
    lane = lax.broadcasted_iota(jnp.int32, (nb, n), 1)
    lane1 = lax.broadcasted_iota(jnp.int32, (nb, 128), 1)
    sub1 = lax.broadcasted_iota(jnp.int32, (nb, 128), 0)
    upper, low = [], []
    for k in range(count):
        off = (k * nb) % 128
        eye = (lane1 == sub1 + off).astype(F32)
        x, e = factor_rows(blocks[k], eye, k * nb, n)
        mine = (lane >= k * nb) & (lane < (k + 1) * nb)
        wide = jnp.concatenate([e] * (n // 128), axis=1)
        t = jnp.where(mine, wide, x)
        urow = lane1[:, :1] * 0 + lax.broadcasted_iota(jnp.int32, (nb, n), 0) + k * nb
        upper.append(jnp.where(lane >= urow, x, 0.0))
        low.append(jnp.where(lane < (k + 1) * nb, t, 0.0))
        if k + 1 < count:
            update = stacked_product(x, t)
            for i in range(k + 1, count):
                blocks[i] = jnp.where(mine, 0.0, blocks[i]) - update[i * nb:(i + 1) * nb]
    return upper, low


def gram_kernel(levels, rows_all, jac_ref, res_ref, gram_ref, data_ref, part, total, *scratch):
    recvs, sums = scratch[:len(levels)], scratch[len(levels):2 * len(levels)]
    rs_send, rs_recv, ag_send, ag_recv = scratch[2 * len(levels):]
    me = lax.axis_index("row")
    places = []
    stride = 1
    for size in levels:
        places.append((lax.rem(me // stride, size), stride, size))
        stride *= size

    def peer(level, step):
        place, stride, size = places[level]
        other = lax.rem(place + step, size)
        return other, me + (other - place) * stride

    barrier = pltpu.get_barrier_semaphore()
    for level, size in enumerate(levels):
        for step in range(1, size):
            pl.semaphore_signal(barrier, inc=1, device_id={"row": peer(level, step)[1]}, device_id_type=pl.DeviceIdType.MESH)

    n = jac_ref.shape[1]
    half = n // 2
    res = res_ref[...]
    first = dot(jac_ref[:, :half], jnp.concatenate([jac_ref[...], res], 1), ((0,), (0,)))
    second = dot(jac_ref[:, half:], jnp.concatenate([jac_ref[:, half:], res], 1), ((0,), (0,)))
    tiles = [first[:, :half], first[:, half:n], second[:, :half], first[:, n:], second[:, half:]]
    for i, tile in enumerate(tiles):
        part[i * half:(i + 1) * half] = tile
    if part.shape[0] > 5 * half:
        part[5 * half:] = jnp.zeros((part.shape[0] - 5 * half, half), F32)
    pl.semaphore_wait(barrier, sum(size - 1 for size in levels))

    source = part
    slot = 0
    for level, size in enumerate(levels):
        seg = source.shape[0] // size
        place = places[level][0]
        copies = []
        for step in range(1, size):
            other, device = peer(level, step)
            copies.append(pltpu.make_async_remote_copy(
                src_ref=source.at[pl.ds(pl.multiple_of(other * seg, 8), seg)],
                dst_ref=recvs[level].at[step - 1],
                send_sem=rs_send.at[slot], recv_sem=rs_recv.at[slot],
                device_id={"row": device}, device_id_type=pl.DeviceIdType.MESH))
            copies[-1].start()
            slot += 1
        value = source[pl.ds(pl.multiple_of(place * seg, 8), seg)]
        for step in range(1, size):
            copies[step - 1].wait_recv()
            value = value + recvs[level][step - 1]
        sums[level][...] = value
        for copy in copies:
            copy.wait_send()
        source = sums[level]

    starts = []
    start = 0
    seg = part.shape[0]
    for place, _, size in places:
        seg //= size
        start = start + place * seg
        starts.append((start, seg))
    total[pl.ds(pl.multiple_of(start, 8), seg)] = source[...]
    slot = 0
    for level in reversed(range(len(levels))):
        start, seg = starts[level]
        mine = total.at[pl.ds(pl.multiple_of(start, 8), seg)]
        copies = []
        for step in range(1, levels[level]):
            copies.append(pltpu.make_async_remote_copy(
                src_ref=mine, dst_ref=mine,
                send_sem=ag_send.at[slot], recv_sem=ag_recv.at[slot],
                device_id={"row": peer(level, step)[1]}, device_id_type=pl.DeviceIdType.MESH))
            copies[-1].start()
            slot += 1
        for copy in copies:
            copy.wait()
    scale = 1.0 / rows_all
    gram_ref[:half, :half] = total[:half] * scale
    gram_ref[:half, half:] = total[half:n] * scale
    gram_ref[half:, :half] = jnp.zeros((half, half), F32)
    gram_ref[half:, half:] = total[n:n + half] * scale
    data_ref[...] = total[n + half:2 * n + half]


def solve_kernel(rows_all, gram_ref, data_ref, jac_ref, basis_ref, upper_ref, update_ref, jac, basis, in_sem, out_sem):
    load = pltpu.make_async_copy(jac_ref, jac, in_sem)
    load.start()
    nb = 32
    n = gram_ref.shape[0]
    blocks = [gram_ref[i * nb:(i + 1) * nb, :] for i in range(n // nb)]
    upper, low = eliminate(blocks, nb)
    for i in range(n // nb):
        upper_ref[i * nb:(i + 1) * nb, :] = upper[i]
    low = jnp.concatenate(low, 0)
    load.wait()
    chunk = jac.shape[0] // 4
    stores = []
    for i in range(4):
        basis[i * chunk:(i + 1) * chunk] = dot(jac[i * chunk:(i + 1) * chunk], low, ((1,), (1,)))
        stores.append(pltpu.make_async_copy(
            basis.at[pl.ds(i * chunk, chunk)], basis_ref.at[pl.ds(i * chunk, chunk)], out_sem.at[i]))
        stores[-1].start()
    projected = dot(low, data_ref[...], ((1,), (0,))) * (1.0 / rows_all ** 0.5)
    update_ref[...] = dot(low, projected, ((0,), (0,)))
    for store in stores:
        store.wait()


def shards(jacobian, residuals):
    devices = lax.axis_size("row")
    rows, n = jacobian.shape
    rhs = residuals.shape[1]
    half = n // 2
    rows_all = rows * devices
    levels = (2, devices // 2)
    unit = 8 * devices
    length = -(-5 * half // unit) * unit
    recvs, sums = [], []
    seg = length
    for size in levels:
        seg //= size
        recvs.append(pltpu.VMEM((size - 1, seg, half), F32))
        sums.append(pltpu.VMEM((seg, half), F32))
    sends = sum(size - 1 for size in levels)
    vmem = pl.BlockSpec(memory_space=pltpu.VMEM)
    hbm = pl.BlockSpec(memory_space=pl.ANY)
    gram, data = pl.pallas_call(
        functools.partial(gram_kernel, levels, rows_all),
        out_shape=(jax.ShapeDtypeStruct((n, n), F32), jax.ShapeDtypeStruct((n, rhs), F32)),
        in_specs=[vmem, vmem],
        out_specs=(vmem, vmem),
        scratch_shapes=[pltpu.VMEM((length, half), F32), pltpu.VMEM((length, half), F32), *recvs, *sums]
        + [pltpu.SemaphoreType.DMA((sends,))] * 4,
        compiler_params=pltpu.CompilerParams(collective_id=0, has_side_effects=True, vmem_limit_bytes=40 * 2 ** 20),
    )(jacobian, residuals)
    return pl.pallas_call(
        functools.partial(solve_kernel, rows_all),
        out_shape=(jax.ShapeDtypeStruct((rows, n), F32), jax.ShapeDtypeStruct((n, n), F32), jax.ShapeDtypeStruct((n, rhs), F32)),
        in_specs=[vmem, vmem, hbm],
        out_specs=(hbm, vmem, vmem),
        scratch_shapes=[pltpu.VMEM((rows, n), F32), pltpu.VMEM((rows, n), F32), pltpu.SemaphoreType.DMA, pltpu.SemaphoreType.DMA((4,))],
        compiler_params=pltpu.CompilerParams(vmem_limit_bytes=40 * 2 ** 20),
    )(gram, data, jacobian)


def solution(mesh):
    return jax.shard_map(
        shards,
        mesh=mesh,
        in_specs=(P(("ens", "row"), None), P(("ens", "row"), None)),
        out_specs=(P(("ens", "row"), None), P("ens", None), P("ens", None)),
        check_vma=False,
    )
```

```python
import functools
import jax
import jax.numpy as jnp
from jax import lax
from jax.experimental import pallas as pl
from jax.experimental.pallas import tpu as pltpu
from jax.sharding import PartitionSpec as P

HI = lax.Precision.HIGHEST
F32 = jnp.float32

def factor_rows(x, extra, first, width):
    nb = x.shape[0]
    diag = []
    mults = []
    rows = [x[8 * i:8 * i + 8] for i in range(nb // 8)]
    ext = [extra[8 * i:8 * i + 8] for i in range(nb // 8)]
    sub = lax.broadcasted_iota(jnp.int32, (8, 128), 0)
    pivots = []
    for p in range(nb // 8):
        cols = []
        for l in range(8):
            c = first + 8 * p + l
            cols.append([jnp.broadcast_to(rows[i][:, c:c + 1], (8, 128)) for i in range(p, nb // 8)])
        pv = jnp.ones((8, 128), F32)
        for j in range(8):
            piv = jnp.broadcast_to(cols[j][0][j:j + 1], (8, 128))
            pv = jnp.where(sub == j, piv, pv)
            r = 1.0 / piv
            f = [cj * r for cj in cols[j]]
            for l in range(j + 1, 8):
                e = jnp.broadcast_to(cols[l][0][j:j + 1], (8, 128))
                cols[l] = [cl - fi * e for cl, fi in zip(cols[l], f)]
            f[0] = jnp.where(sub > j, f[0], 0.0)
            n = rows[0].shape[1]
            xr = jnp.broadcast_to(rows[p][j:j + 1], (8, n))
            er = jnp.broadcast_to(ext[p][j:j + 1], (8, 128))
            for q, fi in enumerate(f):
                rows[p + q] = rows[p + q] - jnp.concatenate([fi] * (n // 128), axis=1) * xr
                ext[p + q] = ext[p + q] - fi * er
        pivots.append(pv)
    out_r, out_e = [], []
    for i in range(nb // 8):
        s = lax.rsqrt(pivots[i])
        n = rows[0].shape[1]
        out_r.append(rows[i] * jnp.concatenate([s] * (n // 128), axis=1))
        out_e.append(ext[i] * s)
    return jnp.concatenate(out_r, 0), jnp.concatenate(out_e, 0)

def dot(a, b, dims, prec=HI):
    return lax.dot_general(a, b, (dims, ((), ())), precision=prec, preferred_element_type=F32)

def split3(x):
    high = x.astype(jnp.bfloat16)
    rest = x - high.astype(F32)
    middle = rest.astype(jnp.bfloat16)
    return high, middle, (rest - middle.astype(F32)).astype(jnp.bfloat16)


def stacked_product(left, right):
    a, b, c = split3(left)
    d, e, f = split3(right)
    return dot(jnp.concatenate([a, a, b, b, a, c], 0), jnp.concatenate([d, e, d, e, f, d], 0), ((0,), (0,)), None)


def eliminate(blocks, nb):
    n = blocks[0].shape[1]
    count = n // nb
    lane = lax.broadcasted_iota(jnp.int32, (nb, n), 1)
    lane1 = lax.broadcasted_iota(jnp.int32, (nb, 128), 1)
    sub1 = lax.broadcasted_iota(jnp.int32, (nb, 128), 0)
    upper, low = [], []
    for k in range(count):
        off = (k * nb) % 128
        eye = (lane1 == sub1 + off).astype(F32)
        x, e = factor_rows(blocks[k], eye, k * nb, n)
        mine = (lane >= k * nb) & (lane < (k + 1) * nb)
        wide = jnp.concatenate([e] * (n // 128), axis=1)
        t = jnp.where(mine, wide, x)
        urow = lane1[:, :1] * 0 + lax.broadcasted_iota(jnp.int32, (nb, n), 0) + k * nb
        upper.append(jnp.where(lane >= urow, x, 0.0))
        low.append(jnp.where(lane < (k + 1) * nb, t, 0.0))
        if k + 1 < count:
            update = stacked_product(x, t)
            for i in range(k + 1, count):
                blocks[i] = jnp.where(mine, 0.0, blocks[i]) - update[i * nb:(i + 1) * nb]
    return upper, low


class Group:
    def __init__(self, levels, part, total, recvs, sums, sems):
        self.levels, self.part, self.total, self.recvs, self.sums = levels, part, total, recvs, sums
        self.sems = sems
        self.me = lax.axis_index("row")
        self.places = []
        stride = 1
        for size in levels:
            self.places.append((lax.rem(self.me // stride, size), stride, size))
            stride *= size

    def peer(self, level, step):
        place, stride, size = self.places[level]
        other = lax.rem(place + step, size)
        return other, self.me + (other - place) * stride

    def steps(self):
        rs_send, rs_recv, ag_send, ag_recv = self.sems
        mesh_id = pl.DeviceIdType.MESH
        pending = []
        source = self.part
        slot = 0
        for level, size in enumerate(self.levels):
            seg = source.shape[0] // size
            place = self.places[level][0]
            copies = []
            for step in range(1, size):
                other, device = self.peer(level, step)
                copies.append(pltpu.make_async_remote_copy(
                    src_ref=source.at[pl.ds(pl.multiple_of(other * seg, 8), seg)],
                    dst_ref=self.recvs[level].at[step - 1],
                    send_sem=rs_send.at[slot], recv_sem=rs_recv.at[slot],
                    device_id={"row": device}, device_id_type=mesh_id))
                copies[-1].start()
                slot += 1
            yield
            value = source[pl.ds(pl.multiple_of(place * seg, 8), seg)]
            for step in range(1, size):
                copies[step - 1].wait_recv()
                value = value + self.recvs[level][step - 1]
            self.sums[level][...] = value
            pending += copies
            source = self.sums[level]
        starts = []
        start = 0
        seg = self.part.shape[0]
        for place, _, size in self.places:
            seg //= size
            start = start + place * seg
            starts.append((start, seg))
        self.total[pl.ds(pl.multiple_of(start, 8), seg)] = source[...]
        slot = 0
        for level in reversed(range(len(self.levels))):
            start, seg = starts[level]
            mine = self.total.at[pl.ds(pl.multiple_of(start, 8), seg)]
            copies = []
            for step in range(1, self.levels[level]):
                copies.append(pltpu.make_async_remote_copy(
                    src_ref=mine, dst_ref=mine,
                    send_sem=ag_send.at[slot], recv_sem=ag_recv.at[slot],
                    device_id={"row": self.peer(level, step)[1]}, device_id_type=mesh_id))
                copies[-1].start()
                slot += 1
            yield
            for copy in copies:
                copy.wait_recv()
            pending += copies
        for copy in pending:
            copy.wait_send()


def scratch_of(levels, length, width):
    shapes = [pltpu.VMEM((length, width), F32), pltpu.VMEM((length, width), F32)]
    recvs, sums = [], []
    seg = length
    for size in levels:
        seg //= size
        recvs.append(pltpu.VMEM((size - 1, seg, width), F32))
        sums.append(pltpu.VMEM((seg, width), F32))
    sends = sum(size - 1 for size in levels)
    return shapes + recvs + sums + [pltpu.SemaphoreType.DMA((sends,))] * 4


def group_of(levels, refs):
    m = len(levels)
    return Group(levels, refs[0], refs[1], refs[2:2 + m], refs[2 + m:2 + 2 * m], refs[2 + 2 * m:])


def gram_kernel(gram_levels, rows_all, jac_ref, res_ref, gram_ref, data_ref, jac, res, in_sem, *scratch):
    cut = 2 + 2 * len(gram_levels) + 4
    grams = group_of(gram_levels, scratch[:cut])
    rows, n = jac.shape
    half = n // 2
    chunk = rows // 4
    loads = []
    for i in range(4):
        piece = pl.ds(i * chunk, chunk)
        loads.append(pltpu.make_async_copy(jac_ref.at[piece], jac.at[piece], in_sem.at[i]))
    loads.append(pltpu.make_async_copy(res_ref, res, in_sem.at[4]))
    for load in loads:
        load.start()

    barrier = pltpu.get_barrier_semaphore()
    count = 0
    for level, size in enumerate(gram_levels):
        for step in range(1, size):
            pl.semaphore_signal(barrier, inc=1, device_id={"row": grams.peer(level, step)[1]}, device_id_type=pl.DeviceIdType.MESH)
            count += 1

    first = jnp.zeros((half, n), F32)
    second = jnp.zeros((half, half), F32)
    for i in range(4):
        loads[i].wait()
        panel = jac[i * chunk:(i + 1) * chunk]
        first = first + dot(panel[:, :half], panel, ((0,), (0,)))
        second = second + dot(panel[:, half:], panel[:, half:], ((0,), (0,)))
    loads[4].wait()
    data = dot(jac[...], res[...], ((0,), (0,)))
    tiles = [first[:, :half], first[:, half:], second, data[:half], data[half:]]
    for i, tile in enumerate(tiles):
        grams.part[i * half:(i + 1) * half] = tile
    if grams.part.shape[0] > 5 * half:
        grams.part[5 * half:] = jnp.zeros((grams.part.shape[0] - 5 * half, half), F32)
    pl.semaphore_wait(barrier, count)
    for _ in grams.steps():
        pass
    total = grams.total
    scale = 1.0 / rows_all
    gram_ref[:half, :half] = total[:half] * scale
    gram_ref[:half, half:] = total[half:n] * scale
    gram_ref[half:, :half] = jnp.zeros((half, half), F32)
    gram_ref[half:, half:] = total[n:n + half] * scale
    data_ref[...] = total[n + half:2 * n + half]


def solve_kernel(rows_all, gram_ref, data_ref, jac_ref, basis_ref, factor_ref, update_ref, jac, basis, factor, update, in_sem, out_sem):
    load = pltpu.make_async_copy(jac_ref, jac, in_sem)
    load.start()
    nb = 32
    n = gram_ref.shape[0]
    blocks = [gram_ref[i * nb:(i + 1) * nb, :] for i in range(n // nb)]
    upper, low = eliminate(blocks, nb)
    for i in range(n // nb):
        factor[i * nb:(i + 1) * nb, :] = upper[i]
    low = jnp.concatenate(low, 0)
    load.wait()
    pieces = 4
    chunk = jac.shape[0] // pieces
    stores = [pltpu.make_async_copy(factor, factor_ref, out_sem.at[pieces])]
    stores[0].start()
    for i in range(pieces):
        piece = pl.ds(i * chunk, chunk)
        basis[i * chunk:(i + 1) * chunk] = dot(jac[i * chunk:(i + 1) * chunk], low, ((1,), (1,)))
        stores.append(pltpu.make_async_copy(basis.at[piece], basis_ref.at[piece], out_sem.at[i]))
        stores[-1].start()
    projected = dot(low, data_ref[...], ((1,), (0,))) * (1.0 / rows_all ** 0.5)
    update[...] = dot(low, projected, ((0,), (0,)))
    stores.append(pltpu.make_async_copy(update, update_ref, out_sem.at[pieces + 1]))
    stores[-1].start()
    for store in stores:
        store.wait()


def shards(jacobian, residuals):
    devices = lax.axis_size("row")
    rows, n = jacobian.shape
    rhs = residuals.shape[1]
    half = n // 2
    rows_all = rows * devices
    gram_levels = (2, devices // 2)
    unit = 8 * devices
    gram_length = -(-5 * half // unit) * unit
    vmem = pl.BlockSpec(memory_space=pltpu.VMEM)
    hbm = pl.BlockSpec(memory_space=pl.ANY)
    square = jax.ShapeDtypeStruct((n, n), F32)
    tall = jax.ShapeDtypeStruct((n, rhs), F32)
    gram, data = pl.pallas_call(
        functools.partial(gram_kernel, gram_levels, rows_all),
        out_shape=(square, tall),
        in_specs=[hbm, hbm],
        out_specs=(vmem, vmem),
        scratch_shapes=[pltpu.VMEM((rows, n), F32), pltpu.VMEM((rows, rhs), F32), pltpu.SemaphoreType.DMA((5,))]
        + scratch_of(gram_levels, gram_length, half),
        compiler_params=pltpu.CompilerParams(collective_id=0, has_side_effects=True, vmem_limit_bytes=40 * 2 ** 20),
    )(jacobian, residuals)
    return pl.pallas_call(
        functools.partial(solve_kernel, rows_all),
        out_shape=(jax.ShapeDtypeStruct((rows, n), F32), square, tall),
        in_specs=[vmem, vmem, hbm],
        out_specs=(hbm, hbm, hbm),
        scratch_shapes=[pltpu.VMEM((rows, n), F32), pltpu.VMEM((rows, n), F32), pltpu.VMEM((n, n), F32), pltpu.VMEM((n, rhs), F32),
                        pltpu.SemaphoreType.DMA, pltpu.SemaphoreType.DMA((6,))],
        compiler_params=pltpu.CompilerParams(vmem_limit_bytes=40 * 2 ** 20),
    )(gram, data, jacobian)


def solution(mesh):
    return jax.shard_map(
        shards,
        mesh=mesh,
        in_specs=(P(("ens", "row"), None), P(("ens", "row"), None)),
        out_specs=(P(("ens", "row"), None), P("ens", None), P("ens", None)),
        check_vma=False,
    )
```
